32 devices in a mesh: feat: 4 (over z), img: 8 (over y, x, core).
Axes of the slice: x: 2, y: 2, z: 4, core: 2. Of those that a mesh axis runs over, the one named last changes fastest.
Arguments:
- features: bfloat16 [448, 61440], P('img', 'feat'), may hold values from -6 to 6
- proj_in: bfloat16 [61440, 768], P('feat', 'img'), may hold values from -0.0234375 to 0.0234375
- proj_out: bfloat16 [768, 512], P('feat'), may hold values from -0.21875 to 0.21875
- centres: bfloat16 [16384, 512], P(('feat', 'img')), may hold values from -0.25 to 0.25
- labels: int32 [448], P('img'), may hold values from 0 to 16383
Outputs:
- centre_grad: float32 [16384, 512], P(('feat', 'img'))
- emb_grad: float32 [448, 512], P('img', 'feat')
The draws below stay inside these ranges and needn't reach their ends.
Inputs may be any that keep to these rules, and one draw needn't show every extreme that they name: `labels`: each image's identity is among the sampled centres, at this position.
All inputs are finite; a program needn't handle non-finite values.
Results may differ from the reference program's by a relative error of at most 0.006.
Values may be sent and summed in bfloat16 or wider, within the bound.
A program may use at most 64 MiB of HBM per device.

```python
import jax
import jax.numpy as jnp
from jax import lax

FEATS = 61440
HID = 768
EMB = 512
CEN_DEV = 512
IMAGES = 448
CENTRES = 16384
N_FEAT = 4
N_IMG = 8


def plant(entries, stream_key, least, high):
    extent = entries.shape
    spot = [jax.random.randint(jax.random.fold_in(stream_key, axis), (), 0, extent[axis]) for axis in range(len(extent))]
    entries = entries.at[tuple(spot)].set(least)
    longest = extent.index(max(extent))
    spot[longest] = (spot[longest] + 1) % extent[longest]
    return entries.at[tuple(spot)].set(high)


def level_of(key, extent, split, least, largest):
    level, own = 1.0, jax.random.fold_in(key, 6)
    for dim, shards_of in split:
        steps = jnp.exp(jax.random.uniform(jax.random.fold_in(own, dim), (shards_of,), jnp.float32, least / len(split), largest / len(split)))
        level = level * jnp.repeat(steps, extent[dim] // shards_of).reshape([-1 if axis == dim else 1 for axis in range(len(extent))])
    return level


def bell_draw(stream_key, extent, spread, limit, pieces=(), kind=jnp.bfloat16):
    result = jax.random.normal(stream_key, extent, jnp.float32) * spread
    if len(pieces) > 0:
        result = level_of(stream_key, extent, pieces, -0.22, 0.18) * result
    return jnp.clip(result, min=-limit, max=limit).astype(kind)


def setup_inputs(seed: int = 0) -> dict:
    key_of = jax.random.split(jax.random.key(seed), 6)
    return {
        "features": bell_draw(key_of[0], (IMAGES, FEATS), 1.0, 6.0, ((0, 8), (1, 4))),
        "proj_in": bell_draw(key_of[1], (FEATS, HID), FEATS ** -0.5, 0.0234375, ((0, 4), (1, 8))),
        "proj_out": bell_draw(key_of[2], (HID, EMB), HID ** -0.5, 0.21875, ((0, 4),)),
        "centres": bell_draw(key_of[3], (CENTRES, EMB), EMB ** -0.5, 0.25, ((0, 32),)),
        "labels": plant(jax.random.randint(key_of[4], (IMAGES,), 0, CENTRES), jax.random.fold_in(key_of[4], 1), 0, CENTRES - 1).astype(jnp.int32),
    }


norm_eps = 1e-06
scale_logit = 64.0
margin_angle = 0.5
sine_floor = 0.04

def reference(features, proj_in, proj_out, centres, labels):
    hidden = jnp.dot(features, proj_in, preferred_element_type=jnp.float32).astype(jnp.bfloat16)
    embed = jnp.dot(hidden, proj_out, preferred_element_type=jnp.float32)
    inverse = lax.rsqrt(lax.optimization_barrier(jnp.sum(embed * embed, axis=1)) + norm_eps)
    unit = embed * inverse[:, None]
    unit_low = unit.astype(jnp.bfloat16)
    count = N_FEAT * N_IMG
    blocks = centres.reshape(count, CEN_DEV, EMB)
    starts = jnp.arange(count, dtype=jnp.int32) * CEN_DEV
    cos_m = jnp.cos(jnp.float32(margin_angle))
    sin_m = jnp.sin(jnp.float32(margin_angle))

    def logits(block, begin):
        wide = block.astype(jnp.float32)
        cinv = lax.rsqrt(lax.optimization_barrier(jnp.sum(wide * wide, axis=1)) + norm_eps)
        unit_centre = wide * cinv[:, None]
        centre_low = unit_centre.astype(jnp.bfloat16)
        cosine = jnp.dot(unit_low, centre_low.T, preferred_element_type=jnp.float32)
        position = begin + jnp.arange(CEN_DEV, dtype=jnp.int32)
        target = labels[:, None] == position[None, :]
        inner = 1.0 - cosine * cosine
        sine = jnp.sqrt(jnp.maximum(inner, sine_floor))
        logit = jnp.where(target, scale_logit * (cosine * cos_m - sine * sin_m), scale_logit * cosine)
        return (cosine, target, inner, sine, jnp.exp(logit), cinv, unit_centre, centre_low)

    def totals(pair):
        return lax.optimization_barrier(jnp.sum(logits(pair[0], pair[1])[4], axis=1))
    total = lax.optimization_barrier(jnp.sum(lax.map(totals, (blocks, starts)), axis=0))

    def backward(carry, pair):
        cosine, target, inner, sine, exps, cinv, unit_centre, centre_low = logits(pair[0], pair[1])
        dlogit = exps / total[:, None] - target.astype(jnp.float32)
        slope = cos_m + jnp.where(inner > sine_floor, sin_m * cosine / sine, 0.0)
        dcos = (dlogit * scale_logit * jnp.where(target, slope, 1.0)).astype(jnp.bfloat16)
        gunit = jnp.dot(dcos.T, unit_low, preferred_element_type=jnp.float32)
        grad = cinv[:, None] * (gunit - unit_centre * lax.optimization_barrier(jnp.sum(unit_centre * gunit, axis=1, keepdims=True)))
        carry = carry + jnp.dot(dcos, centre_low, preferred_element_type=jnp.float32)
        return (carry, grad)
    dunit, grads = lax.scan(backward, jnp.zeros((IMAGES, EMB), jnp.float32), (blocks, starts))
    centre_grad = grads.reshape(CENTRES, EMB)
    emb_grad = inverse[:, None] * (dunit - unit * lax.optimization_barrier(jnp.sum(unit * dunit, axis=1, keepdims=True)))
    return (centre_grad, emb_grad)
```

```python
import functools

import jax
import jax.numpy as jnp
from jax import lax
from jax.experimental import pallas as pl
from jax.experimental.pallas import tpu as pltpu
from jax.sharding import PartitionSpec as P

norm_eps = 1e-06
scale_logit = 64.0
margin_angle = 0.5
sine_floor = 0.04
MESH = pl.DeviceIdType.MESH


def remote(src, dst, send, recv, axis, peer):
    return pltpu.make_async_remote_copy(
        src_ref=src, dst_ref=dst, send_sem=send, recv_sem=recv, device_id={axis: peer}, device_id_type=MESH
    )


def tail(nf, ni, p_ref, po_ref, cen_ref, lab_ref, trig_ref, cg_ref, eg_ref,
         z1, h, lab, u, emb, eo, clow, cosb, tp, tz, msg, rs, zs, zr, uq,
         s1, r1, s2, r2, sl, rl, s4, r4, se, re, s5, r5, s6, r6, s7, r7, s8, r8):
    f, j = lax.axis_index("feat"), lax.axis_index("img")
    images, cols = p_ref.shape
    rows = images // nf
    own = images // ni
    width = cen_ref.shape[1]
    part = width // nf
    zpeer = lambda d: lax.rem(f + d, nf)
    ipeer = lambda d: lax.rem(j + d, ni)

    barrier = pltpu.get_barrier_semaphore()
    for d in range(1, ni):
        pl.semaphore_signal(barrier, inc=1, device_id={"img": ipeer(d)}, device_id_type=MESH)
    for d in range(1, nf):
        pl.semaphore_signal(barrier, inc=1, device_id={"feat": zpeer(d)}, device_id_type=MESH)
    pl.semaphore_wait(barrier, ni + nf - 2)

    sent = []

    def to_feat(src, dst, s, r):
        out = []
        for d in range(1, nf):
            c = remote(src(zpeer(d)), dst(d), s.at[d], r.at[d], "feat", zpeer(d))
            c.start()
            out.append(c)
        sent.extend(out)
        return out

    def to_img(src, dst, s, r):
        out = []
        for d in range(1, ni):
            c = remote(src(ipeer(d)), dst(d), s.at[d], r.at[d], "img", ipeer(d))
            c.start()
            out.append(c)
        sent.extend(out)
        return out

    first = to_feat(lambda g: p_ref.at[pl.ds(pl.multiple_of(g * rows, rows), rows)], lambda d: z1.at[d], s1, r1)
    labs = to_img(lambda c: lab_ref, lambda d: lab.at[d], sl, rl)
    wide = cen_ref[...].astype(jnp.float32)
    cinv = lax.rsqrt(jnp.sum(wide * wide, axis=1, keepdims=True) + norm_eps)
    clow[...] = (wide * cinv).astype(jnp.bfloat16)
    hid = p_ref[pl.ds(pl.multiple_of(f * rows, rows), rows)]
    for d in range(1, nf):
        first[d - 1].wait_recv()
        hid = hid + z1[d]
    h[0] = hid.astype(jnp.bfloat16)

    for c in to_img(lambda c: h.at[0], lambda d: h.at[d], s2, r2):
        c.wait_recv()
    embed = jnp.zeros((rows, width), jnp.float32)
    for c in range(ni):
        slot = lax.rem(j - c + ni, ni)
        embed = embed + jnp.dot(h[slot], po_ref[c], preferred_element_type=jnp.float32)
    emb[...] = embed
    inverse = lax.rsqrt(jnp.sum(embed * embed, axis=1, keepdims=True) + norm_eps)
    u[f] = (embed * inverse).astype(jnp.bfloat16)

    units = to_feat(lambda g: u.at[f], lambda d: u.at[f], s4, r4)
    holder = (j * own) // rows
    offset = pl.multiple_of(lax.rem(j * own, rows), own)
    home = f == holder

    @pl.when(home)
    def _():
        for d in range(1, nf):
            remote(emb.at[pl.ds(offset, own)], eo, se.at[d], re, "feat", zpeer(d)).start()
        eo[...] = emb[pl.ds(offset, own)]

    for d in range(1, nf):
        back = lax.rem(f - d + nf, nf)
        remote(u.at[back], u.at[back], s4.at[d], r4.at[d], "feat", zpeer(d)).wait_recv()
    for c in labs:
        c.wait_recv()
    label = lab_ref[...]
    for d in range(1, ni):
        label = label + lab[d]
    label = label[:1]

    allu = u[...].reshape(images, width)
    cosine = lax.dot_general(clow[...], allu, (((1,), (1,)), ((), ())), preferred_element_type=jnp.float32)
    cen_rows = cen_ref.shape[0]
    begin = (f * ni + j) * cen_rows
    cos_m, sin_m = trig_ref[0], trig_ref[1]

    def forms(cosine):
        position = begin + lax.broadcasted_iota(jnp.int32, cosine.shape, 0)
        target = position == label
        inner = 1.0 - cosine * cosine
        sine = jnp.sqrt(jnp.maximum(inner, sine_floor))
        return target, inner, sine

    target, inner, sine = forms(cosine)
    logit = jnp.where(target, scale_logit * (cosine * cos_m - sine * sin_m), scale_logit * cosine)
    exps = jnp.exp(logit)
    cosb[...] = cosine
    tp[0] = jnp.sum(exps, axis=0, keepdims=True)
    total = tp[0]
    for d, c in enumerate(to_img(lambda c: tp.at[0], lambda d: tp.at[d], s5, r5), 1):
        c.wait_recv()
        total = total + tp[d]
    tz[0] = total
    for d, c in enumerate(to_feat(lambda g: tz.at[0], lambda d: tz.at[d], s6, r6), 1):
        c.wait_recv()
        total = total + tz[d]

    cosine = cosb[...]
    target, inner, sine = forms(cosine)
    logit = jnp.where(target, scale_logit * (cosine * cos_m - sine * sin_m), scale_logit * cosine)
    dlogit = jnp.exp(logit) / total - target.astype(jnp.float32)
    slope = cos_m + jnp.where(inner > sine_floor, sin_m * cosine / sine, 0.0)
    dcos = (dlogit * scale_logit * jnp.where(target, slope, 1.0)).astype(jnp.bfloat16)

    terms = lax.dot_general(dcos, clow[...], (((0,), (0,)), ((), ())), preferred_element_type=jnp.float32)
    half = width // 2
    for c in range(ni):
        block = terms[c * own:(c + 1) * own]
        msg[c] = jnp.concatenate([block[:, :half], block[:, half:]], axis=0).astype(jnp.bfloat16)
    scatter = to_img(lambda c: msg.at[c], lambda d: rs.at[d], s7, r7)

    gunit = jnp.dot(dcos, allu, preferred_element_type=jnp.float32)
    wide = cen_ref[...].astype(jnp.float32)
    cinv = lax.rsqrt(jnp.sum(wide * wide, axis=1, keepdims=True) + norm_eps)
    unit_centre = wide * cinv
    cg_ref[...] = cinv * (gunit - unit_centre * jnp.sum(unit_centre * gunit, axis=1, keepdims=True))

    @pl.when(jnp.logical_not(home))
    def _():
        remote(eo, eo, se.at[0], re, "feat", zpeer(1)).wait_recv()

    mine = eo[...]
    inverse = lax.rsqrt(jnp.sum(mine * mine, axis=1, keepdims=True) + norm_eps)
    unit = mine * inverse
    for g in range(nf):
        uq[g] = unit[:, g * part:(g + 1) * part]
    packed = msg[j].astype(jnp.float32)
    for d in range(1, ni):
        scatter[d - 1].wait_recv()
        packed = packed + rs[d].astype(jnp.float32)
    sums = jnp.concatenate([packed[:own], packed[own:]], axis=1)
    along = jnp.sum(unit * sums, axis=1, keepdims=True)
    for g in range(nf):
        zs[g, :own] = sums[:, g * part:(g + 1) * part]
        zs[g, own:] = jnp.broadcast_to(along, (own, part))
    final = zs[f]
    for d, c in enumerate(to_feat(lambda g: zs.at[g], lambda d: zr.at[d], s8, r8), 1):
        c.wait_recv()
        final = final + zr[d]
    eg_ref[...] = inverse * (final[:own] - uq[f] * final[own:])

    for c in sent:
        c.wait_send()

    @pl.when(home)
    def _():
        for d in range(1, nf):
            remote(emb.at[pl.ds(offset, own)], eo, se.at[d], re, "feat", zpeer(d)).wait_send()


def run_tail(nf, ni, local_cols, all_out, centres, lab_rows, trig):
    images, cols = local_cols.shape
    cen_rows, width = centres.shape
    rows, own, part = images // nf, images // ni, width // nf
    f32, bf16 = jnp.float32, jnp.bfloat16
    dma = pltpu.SemaphoreType.DMA
    vm = pl.BlockSpec(memory_space=pltpu.VMEM)
    return pl.pallas_call(
        functools.partial(tail, nf, ni),
        out_shape=(
            jax.ShapeDtypeStruct((cen_rows, width), f32),
            jax.ShapeDtypeStruct((own, part), f32),
        ),
        in_specs=[vm, vm, vm, vm, pl.BlockSpec(memory_space=pltpu.SMEM)],
        out_specs=(vm, vm),
        scratch_shapes=[
            pltpu.VMEM((nf, rows, cols), f32),
            pltpu.VMEM((ni, rows, cols), bf16),
            pltpu.VMEM((ni,) + lab_rows.shape, jnp.int32),
            pltpu.VMEM((nf, rows, width), bf16),
            pltpu.VMEM((rows, width), f32),
            pltpu.VMEM((own, width), f32),
            pltpu.VMEM((cen_rows, width), bf16),
            pltpu.VMEM((cen_rows, images), f32),
            pltpu.VMEM((ni, 1, images), f32),
            pltpu.VMEM((nf, 1, images), f32),
            pltpu.VMEM((ni, 2 * own, width // 2), bf16),
            pltpu.VMEM((ni, 2 * own, width // 2), bf16),
            pltpu.VMEM((nf, 2 * own, part), f32),
            pltpu.VMEM((nf, 2 * own, part), f32),
            pltpu.VMEM((nf, own, part), f32),
            dma((nf,)), dma((nf,)),
            dma((ni,)), dma((ni,)),
            dma((ni,)), dma((ni,)),
            dma((nf,)), dma((nf,)),
            dma((nf,)), dma(()),
            dma((ni,)), dma((ni,)),
            dma((nf,)), dma((nf,)),
            dma((ni,)), dma((ni,)),
            dma((nf,)), dma((nf,)),
        ],
        compiler_params=pltpu.CompilerParams(
            collective_id=1, has_side_effects=True, vmem_limit_bytes=48 * 1024 * 1024
        ),
    )(local_cols, all_out, centres, lab_rows, trig)


def per_device(features, proj_in, proj_out, centres, labels):
    nf, ni = lax.axis_size("feat"), lax.axis_size("img")
    own = labels.shape[0]
    local_cols = jnp.dot(
        lax.all_gather(features, "img", axis=0, tiled=True),
        proj_in,
        preferred_element_type=jnp.float32,
    )
    all_out = lax.all_gather(proj_out, "feat", axis=0, tiled=True)
    all_out = all_out.reshape(ni, all_out.shape[0] // ni, all_out.shape[1])
    lab_row = lax.dynamic_update_slice(
        jnp.zeros((own * ni,), jnp.int32), labels, (lax.axis_index("img") * own,)
    )
    lab_rows = jnp.broadcast_to(lab_row[None], (8, own * ni))
    trig = jnp.stack([jnp.cos(jnp.float32(margin_angle)), jnp.sin(jnp.float32(margin_angle))])
    return run_tail(nf, ni, local_cols, all_out, centres, lab_rows, trig)


def solution(mesh):
    return jax.shard_map(
        per_device,
        mesh=mesh,
        in_specs=(
            P("img", "feat"),
            P("feat", "img"),
            P("feat", None),
            P(("feat", "img"), None),
            P("img"),
        ),
        out_specs=(P(("feat", "img"), None), P("img", "feat")),
        check_vma=False,
    )
```

```python
import functools
import math

import jax
import jax.numpy as jnp
from jax import lax
from jax.experimental import pallas as pl
from jax.experimental.pallas import tpu as pltpu
from jax.sharding import PartitionSpec as P

norm_eps = 1e-06
scale_logit = 64.0
margin_angle = 0.5
sine_floor = 0.04
MESH = pl.DeviceIdType.MESH


def remote(src, dst, send, recv, axis, peer):
    return pltpu.make_async_remote_copy(
        src_ref=src, dst_ref=dst, send_sem=send, recv_sem=recv, device_id={axis: peer}, device_id_type=MESH
    )


def gather_project(core_j, ni, feat_ref, pin_ref, p_ref, g, b, own_sem, b_sem, sends, recvs, compute):
    j = core_j
    count, _, own, w = g.shape
    mid = count // 2
    core, x, y = lax.rem(j, 2), lax.rem(j // 2, 2), j // 4
    to_s, to_x, to_y = 1 - 2 * core, 2 - 4 * x, 4 - 8 * y
    js, jx, jy = j + to_s, j + to_x, j + to_y
    jd = jx + to_y

    bcopy = pltpu.make_async_copy(pin_ref, b, b_sem)
    bcopy.start()
    cols = lambda k: feat_ref.at[:, k * w:(k + 1) * w]
    mine = [pltpu.make_async_copy(cols(k), g.at[k, j], own_sem.at[k]) for k in range(count)]
    make = lambda kind, k, src, slot, peer: remote(
        src, g.at[k, slot], sends.at[kind, k], recvs.at[kind, k], "img", peer)
    own_x = lambda k: make(0, k, cols(k), j, jx)
    own_y = lambda k: make(1, k, cols(k), j, jy)
    own_s = lambda k: make(2, k, cols(k), j, js)
    diag = lambda k: make(3, k, g.at[k, jx], jx, jy) if k < mid else make(3, k, g.at[k, jy], jy, jx)
    hand_x = lambda k: make(4, k, g.at[k, jx], jx, js)
    hand_y = lambda k: make(5, k, g.at[k, jy], jy, js)
    hand_d = lambda k: make(6, k, g.at[k, jd], jd, js)
    yk = lambda t: (t + mid) % count

    p_ref[...] = jnp.zeros_like(p_ref)
    ahead = 2
    for t in range(ahead):
        own_x(t).start()
        own_y(yk(t)).start()

    def finish(k):
        diag(k).wait_recv()
        hand_d(k).start()

    def project(k):
        mine[k].wait()
        for kind in (2, 4, 5, 6):
            make(kind, k, cols(k), js, js).wait_recv()
        full = g[k].reshape(ni * own, w)
        p_ref[...] += jnp.dot(full, b[k * w:(k + 1) * w], preferred_element_type=jnp.float32)

    for t in range(count):
        k, l = t, yk(t)
        mine[t].start()
        own_s(t).start()
        make(0, k, cols(k), jx, jx).wait_recv()
        if t < mid:
            diag(k).start()
        hand_x(k).start()
        make(1, l, cols(l), jy, jy).wait_recv()
        if t < mid:
            diag(l).start()
        hand_y(l).start()
        if t + ahead < count:
            own_x(k).wait_send()
            own_x(k + ahead).start()
            own_y(l).wait_send()
            own_y(yk(t + ahead)).start()
        if t == 0:
            compute()
            bcopy.wait()
        if 2 <= t < mid + 2:
            finish(t - 2)
            finish(t - 2 + mid)
        if t > mid:
            project(t - mid - 1)
            project(t - 1)
    project(mid - 1)
    project(count - 1)

    def drain():
        for k in range(count):
            if k >= count - ahead:
                own_x(k).wait_send()
            if k in (yk(count - 2), yk(count - 1)):
                own_y(k).wait_send()
            for c in (own_s(k), diag(k), hand_x(k), hand_y(k), hand_d(k)):
                c.wait_send()
    return drain


def tail(nf, ni, fused, *refs):
    if fused:
        feat_ref, pin_ref, po_ref, cen_ref, lab_ref, cg_ref, eg_ref, *refs = refs
        p_ref, g, b, own_sem, b_sem, gs, gr, *refs = refs
    else:
        p_ref, po_ref, cen_ref, lab_ref, cg_ref, eg_ref, *refs = refs
    (z1, po, h, lab, u, emb, eo, clow, cosb, tp, tz, msg, rs, zs, zr, uq,
         s1, r1, s2, r2, sl, rl, s4, r4, se, re, s5, r5, s6, r6, s7, r7, s8, r8, sp, rp) = refs
    f, j = lax.axis_index("feat"), lax.axis_index("img")
    images, cols = p_ref.shape
    rows = images // nf
    own = images // ni
    width = cen_ref.shape[1]
    part = width // nf
    zpeer = lambda d: lax.rem(f + d, nf)
    ipeer = lambda d: lax.rem(j + d, ni)

    barrier = pltpu.get_barrier_semaphore()
    for d in range(1, ni):
        pl.semaphore_signal(barrier, inc=1, device_id={"img": ipeer(d)}, device_id_type=MESH)
    for d in range(1, nf):
        pl.semaphore_signal(barrier, inc=1, device_id={"feat": zpeer(d)}, device_id_type=MESH)
    pl.semaphore_wait(barrier, ni + nf - 2)

    sent = []

    def to_feat(src, dst, s, r):
        out = []
        for d in range(1, nf):
            c = remote(src(zpeer(d)), dst(d), s.at[d], r.at[d], "feat", zpeer(d))
            c.start()
            out.append(c)
        sent.extend(out)
        return out

    def to_img(src, dst, s, r):
        out = []
        for d in range(1, ni):
            c = remote(src(ipeer(d)), dst(d), s.at[d], r.at[d], "img", ipeer(d))
            c.start()
            out.append(c)
        sent.extend(out)
        return out

    outs = to_feat(lambda g: po_ref, lambda d: po.at[f], sp, rp)
    labs = to_img(lambda c: lab_ref, lambda d: lab.at[d], sl, rl)

    def prepare():
        po[f] = po_ref[...]
        lab[0] = lab_ref[...]
        wide = cen_ref[...].astype(jnp.float32)
        cinv = lax.rsqrt(jnp.sum(wide * wide, axis=1, keepdims=True) + norm_eps)
        clow[...] = (wide * cinv).astype(jnp.bfloat16)

    if fused:
        drain = gather_project(j, ni, feat_ref, pin_ref, p_ref, g, b, own_sem, b_sem, gs, gr, prepare)
    else:
        prepare()

    first = to_feat(lambda g: p_ref.at[pl.ds(pl.multiple_of(g * rows, rows), rows)], lambda d: z1.at[d], s1, r1)
    hid = p_ref[pl.ds(pl.multiple_of(f * rows, rows), rows)]
    for d in range(1, nf):
        first[d - 1].wait_recv()
        hid = hid + z1[d]
    h[0] = hid.astype(jnp.bfloat16)

    for c in to_img(lambda c: h.at[0], lambda d: h.at[d], s2, r2):
        c.wait_recv()
    for d in range(1, nf):
        back = lax.rem(f - d + nf, nf)
        remote(po.at[back], po.at[back], sp.at[d], rp.at[d], "feat", zpeer(d)).wait_recv()
    embed = jnp.zeros((rows, width), jnp.float32)
    depth = po_ref.shape[0]
    for c in range(ni):
        slot = lax.rem(j - c + ni, ni)
        at = (c * cols) % depth
        embed = embed + jnp.dot(
            h[slot], po[(c * cols) // depth, at:at + cols], preferred_element_type=jnp.float32
        )
    emb[...] = embed
    inverse = lax.rsqrt(jnp.sum(embed * embed, axis=1, keepdims=True) + norm_eps)
    u[f] = (embed * inverse).astype(jnp.bfloat16)

    units = to_feat(lambda g: u.at[f], lambda d: u.at[f], s4, r4)
    holder = (j * own) // rows
    offset = pl.multiple_of(lax.rem(j * own, rows), own)
    home = f == holder

    @pl.when(home)
    def _():
        for d in range(1, nf):
            remote(emb.at[pl.ds(offset, own)], eo, se.at[d], re, "feat", zpeer(d)).start()
        eo[...] = emb[pl.ds(offset, own)]

    for d in range(1, nf):
        back = lax.rem(f - d + nf, nf)
        remote(u.at[back], u.at[back], s4.at[d], r4.at[d], "feat", zpeer(d)).wait_recv()
    for c in labs:
        c.wait_recv()
    label = jnp.concatenate([lab[lax.rem(j - c + ni, ni)][:1] for c in range(ni)], axis=1)

    allu = u[...].reshape(images, width)
    cosine = lax.dot_general(clow[...], allu, (((1,), (1,)), ((), ())), preferred_element_type=jnp.float32)
    cen_rows = cen_ref.shape[0]
    begin = (f * ni + j) * cen_rows
    cos_m, sin_m = math.cos(margin_angle), math.sin(margin_angle)

    def forms(cosine):
        position = begin + lax.broadcasted_iota(jnp.int32, cosine.shape, 0)
        target = position == label
        inner = 1.0 - cosine * cosine
        sine = jnp.sqrt(jnp.maximum(inner, sine_floor))
        return target, inner, sine

    target, inner, sine = forms(cosine)
    logit = jnp.where(target, scale_logit * (cosine * cos_m - sine * sin_m), scale_logit * cosine)
    exps = jnp.exp(logit)
    cosb[...] = cosine
    tp[0] = jnp.sum(exps, axis=0, keepdims=True)
    total = tp[0]
    for d, c in enumerate(to_img(lambda c: tp.at[0], lambda d: tp.at[d], s5, r5), 1):
        c.wait_recv()
        total = total + tp[d]
    tz[0] = total
    for d, c in enumerate(to_feat(lambda g: tz.at[0], lambda d: tz.at[d], s6, r6), 1):
        c.wait_recv()
        total = total + tz[d]

    cosine = cosb[...]
    target, inner, sine = forms(cosine)
    logit = jnp.where(target, scale_logit * (cosine * cos_m - sine * sin_m), scale_logit * cosine)
    dlogit = jnp.exp(logit) / total - target.astype(jnp.float32)
    slope = cos_m + jnp.where(inner > sine_floor, sin_m * cosine / sine, 0.0)
    dcos = (dlogit * scale_logit * jnp.where(target, slope, 1.0)).astype(jnp.bfloat16)

    terms = lax.dot_general(dcos, clow[...], (((0,), (0,)), ((), ())), preferred_element_type=jnp.float32)
    half = width // 2
    for c in range(ni):
        block = terms[c * own:(c + 1) * own]
        msg[c] = jnp.concatenate([block[:, :half], block[:, half:]], axis=0).astype(jnp.bfloat16)
    scatter = to_img(lambda c: msg.at[c], lambda d: rs.at[d], s7, r7)

    gunit = jnp.dot(dcos, allu, preferred_element_type=jnp.float32)
    wide = cen_ref[...].astype(jnp.float32)
    cinv = lax.rsqrt(jnp.sum(wide * wide, axis=1, keepdims=True) + norm_eps)
    unit_centre = wide * cinv
    cg_ref[...] = cinv * (gunit - unit_centre * jnp.sum(unit_centre * gunit, axis=1, keepdims=True))

    @pl.when(jnp.logical_not(home))
    def _():
        remote(eo, eo, se.at[0], re, "feat", zpeer(1)).wait_recv()

    mine = eo[...]
    inverse = lax.rsqrt(jnp.sum(mine * mine, axis=1, keepdims=True) + norm_eps)
    unit = mine * inverse
    for g in range(nf):
        uq[g] = unit[:, g * part:(g + 1) * part]
    packed = msg[j].astype(jnp.float32)
    for d in range(1, ni):
        scatter[d - 1].wait_recv()
        packed = packed + rs[d].astype(jnp.float32)
    sums = jnp.concatenate([packed[:own], packed[own:]], axis=1)
    along = jnp.sum(unit * sums, axis=1, keepdims=True)
    for g in range(nf):
        zs[g, :own] = sums[:, g * part:(g + 1) * part]
        zs[g, own:] = jnp.broadcast_to(along, (own, part))
    final = zs[f]
    for d, c in enumerate(to_feat(lambda g: zs.at[g], lambda d: zr.at[d], s8, r8), 1):
        c.wait_recv()
        final = final + zr[d]
    eg_ref[...] = inverse * (final[:own] - uq[f] * final[own:])

    for c in sent:
        c.wait_send()
    if fused:
        drain()

    @pl.when(home)
    def _():
        for d in range(1, nf):
            remote(emb.at[pl.ds(offset, own)], eo, se.at[d], re, "feat", zpeer(d)).wait_send()


def chunks_of(width):
    for count in (12, 10, 8, 6, 4, 2):
        if width % (count * 128) == 0:
            return count
    return 0


def run_tail(nf, ni, firsts, proj_out, centres, lab_rows):
    fused = len(firsts) == 2
    own = lab_rows.shape[1]
    images = own * ni
    cols = firsts[-1].shape[1]
    cen_rows, width = centres.shape
    rows, part = images // nf, width // nf
    f32, bf16 = jnp.float32, jnp.bfloat16
    dma = pltpu.SemaphoreType.DMA
    vm = pl.BlockSpec(memory_space=pltpu.VMEM)
    hbm = pl.BlockSpec(memory_space=pl.ANY)
    scratch = []
    if fused:
        count = chunks_of(firsts[0].shape[1])
        scratch = [
            pltpu.VMEM((images, cols), f32),
            pltpu.VMEM((count, ni, own, firsts[0].shape[1] // count), bf16),
            pltpu.VMEM(firsts[1].shape, bf16),
            dma((count,)), dma(()), dma((7, count)), dma((7, count)),
        ]
    return pl.pallas_call(
        functools.partial(tail, nf, ni, fused),
        out_shape=(
            jax.ShapeDtypeStruct((cen_rows, width), f32),
            jax.ShapeDtypeStruct((own, part), f32),
        ),
        in_specs=([hbm, hbm] if fused else [vm]) + [vm, vm, vm],
        out_specs=(vm, vm),
        scratch_shapes=scratch + [
            pltpu.VMEM((nf, rows, cols), f32),
            pltpu.VMEM((nf,) + proj_out.shape, bf16),
            pltpu.VMEM((ni, rows, cols), bf16),
            pltpu.VMEM((ni,) + lab_rows.shape, jnp.int32),
            pltpu.VMEM((nf, rows, width), bf16),
            pltpu.VMEM((rows, width), f32),
            pltpu.VMEM((own, width), f32),
            pltpu.VMEM((cen_rows, width), bf16),
            pltpu.VMEM((cen_rows, images), f32),
            pltpu.VMEM((ni, 1, images), f32),
            pltpu.VMEM((nf, 1, images), f32),
            pltpu.VMEM((ni, 2 * own, width // 2), bf16),
            pltpu.VMEM((ni, 2 * own, width // 2), bf16),
            pltpu.VMEM((nf, 2 * own, part), f32),
            pltpu.VMEM((nf, 2 * own, part), f32),
            pltpu.VMEM((nf, own, part), f32),
            dma((nf,)), dma((nf,)),
            dma((ni,)), dma((ni,)),
            dma((ni,)), dma((ni,)),
            dma((nf,)), dma((nf,)),
            dma((nf,)), dma(()),
            dma((ni,)), dma((ni,)),
            dma((nf,)), dma((nf,)),
            dma((ni,)), dma((ni,)),
            dma((nf,)), dma((nf,)),
            dma((nf,)), dma((nf,)),
        ],
        compiler_params=pltpu.CompilerParams(
            collective_id=1, has_side_effects=True, vmem_limit_bytes=56 * 1024 * 1024
        ),
    )(*firsts, proj_out, centres, lab_rows)


def per_device(features, proj_in, proj_out, centres, labels):
    nf, ni = lax.axis_size("feat"), lax.axis_size("img")
    if ni == 2 * 2 * 2 and chunks_of(features.shape[1]):
        firsts = (features, proj_in)
    else:
        everything = lax.all_gather(features, "img", axis=0, tiled=True)
        firsts = (jnp.dot(everything, proj_in, preferred_element_type=jnp.float32),)
    lab_rows = jnp.broadcast_to(labels[None], (8, labels.shape[0]))
    return run_tail(nf, ni, firsts, proj_out, centres, lab_rows)


def solution(mesh):
    return jax.shard_map(
        per_device,
        mesh=mesh,
        in_specs=(
            P("img", "feat"),
            P("feat", "img"),
            P("feat", None),
            P(("feat", "img"), None),
            P("img"),
        ),
        out_specs=(P(("feat", "img"), None), P("img", "feat")),
        check_vma=False,
    )
```

```python
import functools
import math

import jax
import jax.numpy as jnp
from jax import lax
from jax.experimental import pallas as pl
from jax.experimental.pallas import tpu as pltpu
from jax.sharding import PartitionSpec as P

norm_eps = 1e-06
scale_logit = 64.0
margin_angle = 0.5
sine_floor = 0.04
MESH = pl.DeviceIdType.MESH


def remote(src, dst, send, recv, axis, peer):
    return pltpu.make_async_remote_copy(
        src_ref=src, dst_ref=dst, send_sem=send, recv_sem=recv, device_id={axis: peer}, device_id_type=MESH
    )


def gather_project(core_j, ni, feat_ref, pin_ref, p_ref, g, b, own_sem, b_sem, sends, recvs, compute):
    j = core_j
    count, _, own, w = g.shape
    mid = count // 2
    core, x, y = lax.rem(j, 2), lax.rem(j // 2, 2), j // 4
    to_s, to_x, to_y = 1 - 2 * core, 2 - 4 * x, 4 - 8 * y
    js, jx, jy = j + to_s, j + to_x, j + to_y
    jd = jx + to_y

    bcopy = pltpu.make_async_copy(pin_ref, b, b_sem)
    bcopy.start()
    cols = lambda k: feat_ref.at[:, k * w:(k + 1) * w]
    mine = [pltpu.make_async_copy(cols(k), g.at[k, j], own_sem.at[k]) for k in range(count)]
    make = lambda kind, k, src, slot, peer: remote(
        src, g.at[k, slot], sends.at[kind, k], recvs.at[kind, k], "img", peer)
    own_x = lambda k: make(0, k, cols(k), j, jx)
    own_y = lambda k: make(1, k, cols(k), j, jy)
    own_s = lambda k: make(2, k, cols(k), j, js)
    diag = lambda k: make(3, k, g.at[k, jx], jx, jy) if k < mid else make(3, k, g.at[k, jy], jy, jx)
    hand_x = lambda k: make(4, k, g.at[k, jx], jx, js)
    hand_y = lambda k: make(5, k, g.at[k, jy], jy, js)
    hand_d = lambda k: make(6, k, g.at[k, jd], jd, js)
    yk = lambda t: (t + mid) % count

    p_ref[...] = jnp.zeros_like(p_ref)
    ahead = 2
    for t in range(ahead):
        own_x(t).start()
        own_y(yk(t)).start()

    def finish(k):
        diag(k).wait_recv()
        hand_d(k).start()

    def project(k):
        mine[k].wait()
        for kind in (2, 4, 5, 6):
            make(kind, k, cols(k), js, js).wait_recv()
        full = g[k].reshape(ni * own, w)
        p_ref[...] += jnp.dot(full, b[k * w:(k + 1) * w], preferred_element_type=jnp.float32)

    for t in range(count):
        k, l = t, yk(t)
        mine[t].start()
        own_s(t).start()
        make(0, k, cols(k), jx, jx).wait_recv()
        if t < mid:
            diag(k).start()
        hand_x(k).start()
        make(1, l, cols(l), jy, jy).wait_recv()
        if t < mid:
            diag(l).start()
        hand_y(l).start()
        if t + ahead < count:
            own_x(k).wait_send()
            own_x(k + ahead).start()
            own_y(l).wait_send()
            own_y(yk(t + ahead)).start()
        if t == 0:
            compute()
            bcopy.wait()
        if 2 <= t < mid + 2:
            finish(t - 2)
            finish(t - 2 + mid)
        if t > mid:
            project(t - mid - 1)
            project(t - 1)
    project(mid - 1)
    project(count - 1)

    def drain():
        for k in range(count):
            if k >= count - ahead:
                own_x(k).wait_send()
            if k in (yk(count - 2), yk(count - 1)):
                own_y(k).wait_send()
            for c in (own_s(k), diag(k), hand_x(k), hand_y(k), hand_d(k)):
                c.wait_send()
    return drain


def tail(nf, ni, fused, *refs):
    if fused:
        feat_ref, pin_ref, po_ref, cen_ref, lab_ref, cg_ref, eg_ref, *refs = refs
        p_ref, g, b, own_sem, b_sem, gs, gr, *refs = refs
    else:
        p_ref, po_ref, cen_ref, lab_ref, cg_ref, eg_ref, *refs = refs
    (z1, po, h, lab, u, emb, eo, clow, cosb, tp, tz, msg, rs, zs, zr, uq,
         s1, r1, s2, r2, sl, rl, s4, r4, se, re, s5, r5, s6, r6, s7, r7, s8, r8, sp, rp, sh, rh) = refs
    f, j = lax.axis_index("feat"), lax.axis_index("img")
    images, cols = p_ref.shape
    rows = images // nf
    own = images // ni
    width = cen_ref.shape[1]
    part = width // nf
    zpeer = lambda d: lax.rem(f + d, nf)
    ipeer = lambda d: lax.rem(j + d, ni)

    barrier = pltpu.get_barrier_semaphore()
    for d in range(1, ni):
        pl.semaphore_signal(barrier, inc=1, device_id={"img": ipeer(d)}, device_id_type=MESH)
    for d in range(1, nf):
        pl.semaphore_signal(barrier, inc=1, device_id={"feat": zpeer(d)}, device_id_type=MESH)
    pl.semaphore_wait(barrier, ni + nf - 2)

    sent = []

    def to_feat(src, dst, s, r):
        out = []
        for d in range(1, nf):
            c = remote(src(zpeer(d)), dst(d), s.at[d], r.at[d], "feat", zpeer(d))
            c.start()
            out.append(c)
        sent.extend(out)
        return out

    def to_img(src, dst, s, r):
        out = []
        for d in range(1, ni):
            c = remote(src(ipeer(d)), dst(d), s.at[d], r.at[d], "img", ipeer(d))
            c.start()
            out.append(c)
        sent.extend(out)
        return out

    outs = to_feat(lambda g: po_ref, lambda d: po.at[f], sp, rp)
    labs = to_img(lambda c: lab_ref, lambda d: lab.at[d], sl, rl)

    def prepare():
        po[f] = po_ref[...]
        lab[0] = lab_ref[...]
        wide = cen_ref[...].astype(jnp.float32)
        cinv = lax.rsqrt(jnp.sum(wide * wide, axis=1, keepdims=True) + norm_eps)
        clow[...] = (wide * cinv).astype(jnp.bfloat16)

    if fused:
        drain = gather_project(j, ni, feat_ref, pin_ref, p_ref, g, b, own_sem, b_sem, gs, gr, prepare)
    else:
        prepare()

    first = to_feat(lambda g: p_ref.at[pl.ds(pl.multiple_of(g * rows, rows), rows)], lambda d: z1.at[d], s1, r1)
    hid = p_ref[pl.ds(pl.multiple_of(f * rows, rows), rows)]
    for d in range(1, nf):
        first[d - 1].wait_recv()
        hid = hid + z1[d]
    h[0] = hid.astype(jnp.bfloat16)

    for c in to_img(lambda c: h.at[0], lambda d: h.at[d], s2, r2):
        c.wait_recv()
    for d in range(1, nf):
        back = lax.rem(f - d + nf, nf)
        remote(po.at[back], po.at[back], sp.at[d], rp.at[d], "feat", zpeer(d)).wait_recv()
    embed = jnp.zeros((rows, width), jnp.float32)
    depth = po_ref.shape[0]
    for c in range(ni):
        slot = lax.rem(j - c + ni, ni)
        at = (c * cols) % depth
        embed = embed + jnp.dot(
            h[slot], po[(c * cols) // depth, at:at + cols], preferred_element_type=jnp.float32
        )
    emb[...] = embed
    inverse = lax.rsqrt(jnp.sum(embed * embed, axis=1, keepdims=True) + norm_eps)

    side = lax.rem(j, 2)
    half = width // 2
    low = (embed * inverse).astype(jnp.bfloat16)
    u[0, f] = low[:, :half]
    u[1, f] = low[:, half:]
    units = to_feat(lambda g: u.at[side, f], lambda d: u.at[side, f], s4, r4)
    sibling = j + 1 - 2 * side
    hands = []
    for d in range(1, nf):
        back = lax.rem(f - d + nf, nf)
        remote(u.at[side, back], u.at[side, back], s4.at[d], r4.at[d], "feat", zpeer(d)).wait_recv()
        c = remote(u.at[side, back], u.at[side, back], sh.at[d], rh.at[d], "img", sibling)
        c.start()
        hands.append(c)
    sent.extend(hands)
    holder = (j * own) // rows
    offset = pl.multiple_of(lax.rem(j * own, rows), own)
    home = f == holder

    @pl.when(home)
    def _():
        for d in range(1, nf):
            remote(emb.at[pl.ds(offset, own)], eo, se.at[d], re, "feat", zpeer(d)).start()
        eo[...] = emb[pl.ds(offset, own)]

    for d in range(1, nf):
        back = lax.rem(f - d + nf, nf)
        remote(u.at[1 - side, back], u.at[1 - side, back], sh.at[d], rh.at[d], "img", sibling).wait_recv()
    for c in labs:
        c.wait_recv()
    label = jnp.concatenate([lab[lax.rem(j - c + ni, ni)][:1] for c in range(ni)], axis=1)

    allu = jnp.concatenate([u[0].reshape(images, half), u[1].reshape(images, half)], axis=1)
    cosine = lax.dot_general(clow[...], allu, (((1,), (1,)), ((), ())), preferred_element_type=jnp.float32)
    cen_rows = cen_ref.shape[0]
    begin = (f * ni + j) * cen_rows
    cos_m, sin_m = math.cos(margin_angle), math.sin(margin_angle)

    def forms(cosine):
        position = begin + lax.broadcasted_iota(jnp.int32, cosine.shape, 0)
        target = position == label
        inner = 1.0 - cosine * cosine
        sine = jnp.sqrt(jnp.maximum(inner, sine_floor))
        return target, inner, sine

    target, inner, sine = forms(cosine)
    logit = jnp.where(target, scale_logit * (cosine * cos_m - sine * sin_m), scale_logit * cosine)
    exps = jnp.exp(logit)
    cosb[...] = cosine
    tp[0] = jnp.sum(exps, axis=0, keepdims=True)
    total = tp[0]
    for d, c in enumerate(to_img(lambda c: tp.at[0], lambda d: tp.at[d], s5, r5), 1):
        c.wait_recv()
        total = total + tp[d]
    tz[0] = total
    for d, c in enumerate(to_feat(lambda g: tz.at[0], lambda d: tz.at[d], s6, r6), 1):
        c.wait_recv()
        total = total + tz[d]

    cosine = cosb[...]
    target, inner, sine = forms(cosine)
    logit = jnp.where(target, scale_logit * (cosine * cos_m - sine * sin_m), scale_logit * cosine)
    dlogit = jnp.exp(logit) / total - target.astype(jnp.float32)
    slope = cos_m + jnp.where(inner > sine_floor, sin_m * cosine / sine, 0.0)
    dcos = (dlogit * scale_logit * jnp.where(target, slope, 1.0)).astype(jnp.bfloat16)

    terms = lax.dot_general(dcos, clow[...], (((0,), (0,)), ((), ())), preferred_element_type=jnp.float32)
    for c in range(ni):
        block = terms[c * own:(c + 1) * own]
        msg[c] = jnp.concatenate([block[:, :half], block[:, half:]], axis=0).astype(jnp.bfloat16)
    scatter = to_img(lambda c: msg.at[c], lambda d: rs.at[d], s7, r7)

    gunit = jnp.dot(dcos, allu, preferred_element_type=jnp.float32)
    wide = cen_ref[...].astype(jnp.float32)
    cinv = lax.rsqrt(jnp.sum(wide * wide, axis=1, keepdims=True) + norm_eps)
    unit_centre = wide * cinv
    cg_ref[...] = cinv * (gunit - unit_centre * jnp.sum(unit_centre * gunit, axis=1, keepdims=True))

    @pl.when(jnp.logical_not(home))
    def _():
        remote(eo, eo, se.at[0], re, "feat", zpeer(1)).wait_recv()

    mine = eo[...]
    inverse = lax.rsqrt(jnp.sum(mine * mine, axis=1, keepdims=True) + norm_eps)
    unit = mine * inverse
    for g in range(nf):
        uq[g] = unit[:, g * part:(g + 1) * part]
    packed = msg[j].astype(jnp.float32)
    for d in range(1, ni):
        scatter[d - 1].wait_recv()
        packed = packed + rs[d].astype(jnp.float32)
    sums = jnp.concatenate([packed[:own], packed[own:]], axis=1)
    along = jnp.sum(unit * sums, axis=1, keepdims=True)
    for g in range(nf):
        zs[g, :own] = sums[:, g * part:(g + 1) * part]
        zs[g, own:] = jnp.broadcast_to(along, (own, part))
    final = zs[f]
    for d, c in enumerate(to_feat(lambda g: zs.at[g], lambda d: zr.at[d], s8, r8), 1):
        c.wait_recv()
        final = final + zr[d]
    eg_ref[...] = inverse * (final[:own] - uq[f] * final[own:])

    for c in sent:
        c.wait_send()
    if fused:
        drain()

    @pl.when(home)
    def _():
        for d in range(1, nf):
            remote(emb.at[pl.ds(offset, own)], eo, se.at[d], re, "feat", zpeer(d)).wait_send()


def chunks_of(width):
    for count in (12, 10, 8, 6, 4, 2):
        if width % (count * 128) == 0:
            return count
    return 0


def run_tail(nf, ni, firsts, proj_out, centres, lab_rows):
    fused = len(firsts) == 2
    own = lab_rows.shape[1]
    images = own * ni
    cols = firsts[-1].shape[1]
    cen_rows, width = centres.shape
    rows, part = images // nf, width // nf
    f32, bf16 = jnp.float32, jnp.bfloat16
    dma = pltpu.SemaphoreType.DMA
    vm = pl.BlockSpec(memory_space=pltpu.VMEM)
    hbm = pl.BlockSpec(memory_space=pl.ANY)
    scratch = []
    if fused:
        count = chunks_of(firsts[0].shape[1])
        scratch = [
            pltpu.VMEM((images, cols), f32),
            pltpu.VMEM((count, ni, own, firsts[0].shape[1] // count), bf16),
            pltpu.VMEM(firsts[1].shape, bf16),
            dma((count,)), dma(()), dma((7, count)), dma((7, count)),
        ]
    return pl.pallas_call(
        functools.partial(tail, nf, ni, fused),
        out_shape=(
            jax.ShapeDtypeStruct((cen_rows, width), f32),
            jax.ShapeDtypeStruct((own, part), f32),
        ),
        in_specs=([hbm, hbm] if fused else [vm]) + [vm, vm, vm],
        out_specs=(vm, vm),
        scratch_shapes=scratch + [
            pltpu.VMEM((nf, rows, cols), f32),
            pltpu.VMEM((nf,) + proj_out.shape, bf16),
            pltpu.VMEM((ni, rows, cols), bf16),
            pltpu.VMEM((ni,) + lab_rows.shape, jnp.int32),
            pltpu.VMEM((2, nf, rows, width // 2), bf16),
            pltpu.VMEM((rows, width), f32),
            pltpu.VMEM((own, width), f32),
            pltpu.VMEM((cen_rows, width), bf16),
            pltpu.VMEM((cen_rows, images), f32),
            pltpu.VMEM((ni, 1, images), f32),
            pltpu.VMEM((nf, 1, images), f32),
            pltpu.VMEM((ni, 2 * own, width // 2), bf16),
            pltpu.VMEM((ni, 2 * own, width // 2), bf16),
            pltpu.VMEM((nf, 2 * own, part), f32),
            pltpu.VMEM((nf, 2 * own, part), f32),
            pltpu.VMEM((nf, own, part), f32),
            dma((nf,)), dma((nf,)),
            dma((ni,)), dma((ni,)),
            dma((ni,)), dma((ni,)),
            dma((nf,)), dma((nf,)),
            dma((nf,)), dma(()),
            dma((ni,)), dma((ni,)),
            dma((nf,)), dma((nf,)),
            dma((ni,)), dma((ni,)),
            dma((nf,)), dma((nf,)),
            dma((nf,)), dma((nf,)),
            dma((nf,)), dma((nf,)),
        ],
        compiler_params=pltpu.CompilerParams(
            collective_id=1, has_side_effects=True, vmem_limit_bytes=56 * 1024 * 1024
        ),
    )(*firsts, proj_out, centres, lab_rows)


def per_device(features, proj_in, proj_out, centres, labels):
    nf, ni = lax.axis_size("feat"), lax.axis_size("img")
    if ni == 2 * 2 * 2 and chunks_of(features.shape[1]):
        firsts = (features, proj_in)
    else:
        everything = lax.all_gather(features, "img", axis=0, tiled=True)
        firsts = (jnp.dot(everything, proj_in, preferred_element_type=jnp.float32),)
    lab_rows = jnp.broadcast_to(labels[None], (8, labels.shape[0]))
    return run_tail(nf, ni, firsts, proj_out, centres, lab_rows)


def solution(mesh):
    return jax.shard_map(
        per_device,
        mesh=mesh,
        in_specs=(
            P("img", "feat"),
            P("feat", "img"),
            P("feat", None),
            P(("feat", "img"), None),
            P("img"),
        ),
        out_specs=(P(("feat", "img"), None), P("img", "feat")),
        check_vma=False,
    )
```
